512 devices in a mesh: leaf: 64 (over z, y), grp: 8 (over x, core).
Axes of the slice: x: 4, y: 8, z: 8, core: 2. Of those that a mesh axis runs over, the one named last changes fastest.
Arguments:
- vectors: bfloat16 [4096, 256, 16], P(('leaf', 'grp')), may hold values from -6 to 6
- leaf_basis: bfloat16 [4096, 256, 64], P(('leaf', 'grp')), may hold values from -0.375 to 0.375
- transfer: float32 [512, 15, 64, 64], P(('leaf', 'grp')), may hold values from -0.5 to 0.5
- couple_src: int32 [512, 12, 3], P(('leaf', 'grp')), may hold values from 0 to 4095, as said below
- couple_mat: float32 [512, 12, 3, 64, 64], P(('leaf', 'grp')), may hold values from -0.4375 to 0.4375
- root_src: int32 [64, 4], P('leaf'), may hold values from 0 to 63, as said below
- root_mat: float32 [64, 4, 64, 64], P('leaf'), may hold values from -0.375 to 0.375
- near_src: int32 [4096, 3], P(('leaf', 'grp')), may hold values from 0 to 4095, as said below
- near_blocks: bfloat16 [4096, 256, 3, 256], P(('leaf', 'grp')), may hold values from -0.21875 to 0.21875
Outputs:
- product: float32 [4096, 256, 16], P(('leaf', 'grp'))
The draws below stay inside these ranges and needn't reach their ends.
Inputs may be any that keep to these rules, and one draw needn't show every extreme that they name: `couple_src`: rows of each block d hold the levels 0, 1, ... in order, 8, 4, ... rows down to 4; entry [d, r, j] names a cluster of row r's level 2 or 3 places from row r's cluster on the cycle of that level's clusters (the last followed by the first); a row's three entries are distinct. `root_src`: each entry names another top cluster neither equal nor next to the row's own on the cycle of 64 top clusters; a row's entries are distinct. `near_src`: entry [t, 0] is t itself; the other two are distinct leaves 1 or 2 places from t on the cycle of 4096 leaves.
All inputs are finite; a program needn't handle non-finite values.
Results may differ from the reference program's by a relative error of at most 0.0019.
Values may be sent and summed in bfloat16 or wider, within the bound.
A program may use at most 64 MiB of HBM per device.

```python
import jax
import jax.numpy as jnp
import numpy as np
from jax import lax

RANK = 64
NV = 16
LEAF = 256
LOCAL = 3
NC = 3
NN = 3
NR = 4
SUBTREES = 64
LEAVES = 4096
COUPLED = 12
TRANSFERS = 15
DEVICES = 512


def draw_couple_src(key, part):
    key = jax.random.fold_in(key, 11)
    per_device = 2 ** LOCAL
    widths = []
    positions = []
    for height in range(LOCAL - 1):
        clusters = per_device >> height
        widths += [clusters] * clusters
        positions += list(range(clusters))
    width_row = jnp.asarray(np.array(widths, np.int32))
    place_row = jnp.asarray(np.array(positions, np.int32))
    owners = jnp.arange(DEVICES, dtype=jnp.int32)[:, None]
    targets = owners * width_row[None, :] + place_row[None, :]
    dropped = jax.random.randint(key, (DEVICES, 2 * per_device - 4), 0, 4)
    dropped = dropped.at[0, 2:4].set(3)
    options = jnp.array([[-2, 2, 3], [-3, 2, 3], [-3, -2, 3], [-3, -2, 2]], jnp.int32)
    offsets = options[dropped]
    return jnp.mod(targets[:, :, None] + offsets, (width_row * DEVICES)[None, :, None]).astype(jnp.int32)


def draw_root_src(key, part):
    key = jax.random.fold_in(key, 37)
    candidates = SUBTREES - 3
    scores = jax.random.randint(key, (SUBTREES, candidates), 0, 1 << 20)
    scores = scores * candidates + jnp.arange(candidates, dtype=jnp.int32)[None, :]
    scores = scores.at[1:3, candidates - 1].set(-1)
    order = jnp.argsort(scores, axis=1, stable=True)[:, :NR]
    owners = jnp.arange(SUBTREES, dtype=jnp.int32)[:, None]
    return jnp.mod(owners + 2 + order.astype(jnp.int32), SUBTREES).astype(jnp.int32)


def draw_near_src(key, part):
    key = jax.random.fold_in(key, 23)
    total = LEAVES
    chosen = jax.random.randint(key, (total,), 0, 6)
    chosen = chosen.at[0].set(2)
    pairs = jnp.array([[-2, -1], [-2, 1], [-2, 2], [-1, 1], [-1, 2], [1, 2]], jnp.int32)
    leaves = jnp.arange(total, dtype=jnp.int32)[:, None]
    offsets = jnp.concatenate([jnp.zeros((total, 1), jnp.int32), pairs[chosen]], axis=1)
    return jnp.mod(leaves + offsets, total).astype(jnp.int32)


def shard_levels(key, dims, cuts, smallest, top_value):
    def one(axis_at, shards_of):
        steps = jax.random.uniform(jax.random.fold_in(jax.random.fold_in(key, 6), axis_at), (shards_of,), jnp.float32, smallest / len(cuts), top_value / len(cuts))
        return jnp.repeat(jnp.exp(steps), dims[axis_at] // shards_of).reshape((-1,) + (1,) * (len(dims) - axis_at - 1))

    factor_of = one(*cuts[0])
    for cut in cuts[1:]:
        factor_of = factor_of * one(*cut)
    return factor_of


def gaussian(rng, dims, scale, reach, split=(), kind=jnp.bfloat16):
    result = scale * jax.random.normal(rng, dims, jnp.float32)
    if split:
        result = result * shard_levels(rng, dims, split, -0.22, 0.18)
    return jnp.clip(result, -reach, reach).astype(kind)


def setup_inputs(seed: int = 0) -> dict:
    key_list = jax.random.split(jax.random.key(seed), 10)
    vectors = gaussian(key_list[0], (LEAVES, LEAF, NV), 1.0, 6.0, ((0, 512),))
    leaf_basis = gaussian(key_list[1], (LEAVES, LEAF, RANK), LEAF ** -0.5, 0.375, ((0, 512),))
    transfer = gaussian(key_list[2], (DEVICES, TRANSFERS, RANK, RANK), (2 * RANK) ** -0.5, 0.5, ((0, 512),), jnp.float32)
    couple_src = draw_couple_src(jax.random.fold_in(key_list[9], 71), 0)
    couple_mat = gaussian(key_list[4], (DEVICES, COUPLED, NC, RANK, RANK), (NC * RANK) ** -0.5, 0.4375, ((0, 512),), jnp.float32)
    root_src = draw_root_src(jax.random.fold_in(key_list[9], 71), 0)
    root_mat = gaussian(key_list[6], (SUBTREES, NR, RANK, RANK), (NR * RANK) ** -0.5, 0.375, ((0, 64),), jnp.float32)
    near_src = draw_near_src(jax.random.fold_in(key_list[9], 71), 0)
    near_blocks = gaussian(key_list[8], (LEAVES, LEAF, NN, LEAF), (NN * LEAF) ** -0.5, 0.21875, ((0, 512),))
    return {"vectors": vectors, "leaf_basis": leaf_basis, "transfer": transfer, "couple_src": couple_src, "couple_mat": couple_mat, "root_src": root_src, "root_mat": root_mat, "near_src": near_src, "near_blocks": near_blocks}


highest = lax.Precision.HIGHEST


def reference(vectors, leaf_basis, transfer, couple_src, couple_mat, root_src, root_mat, near_src, near_blocks):
    per_device = 2 ** LOCAL
    coeffs = [jnp.einsum("tmv,tmk->tvk", vectors.astype(jnp.float32), leaf_basis.astype(jnp.float32), precision=highest)]
    for height in range(1, LOCAL + 1):
        clusters = per_device >> (height - 1)
        offset = 2 * per_device - 2 * clusters
        matrices = transfer[:, offset:offset + clusters].reshape(-1, RANK, RANK)
        children = jnp.einsum("cvk,ckl->cvl", coeffs[-1], matrices, precision=highest)
        coeffs.append(children.reshape(-1, 2, NV, RANK).sum(axis=1))
    device_up = transfer[:, 2 * per_device - 2]
    lifted = jnp.einsum("dvk,dkl->dvl", coeffs[LOCAL], device_up, precision=highest)
    tops = lifted.reshape(SUBTREES, -1, NV, RANK).sum(axis=1)
    couplings = []
    for height in range(LOCAL - 1):
        clusters = per_device >> height
        offset = 2 * per_device - 2 * clusters
        sources = couple_src[:, offset:offset + clusters].reshape(-1, NC)
        blocks = couple_mat[:, offset:offset + clusters].reshape(-1, NC, RANK, RANK)
        picked = coeffs[height][sources]
        couplings.append(jnp.einsum("tcvk,tckl->tvl", picked, blocks, precision=highest))
    top_down = jnp.einsum("rcvk,rckl->rvl", tops[root_src], root_mat, precision=highest)
    spread_top = jnp.repeat(top_down, lifted.shape[0] // SUBTREES, axis=0)
    downward = jnp.einsum("dvl,dkl->dvk", spread_top, device_up, precision=highest)
    for height in range(LOCAL, 0, -1):
        clusters = per_device >> (height - 1)
        offset = 2 * per_device - 2 * clusters
        matrices = transfer[:, offset:offset + clusters].reshape(-1, RANK, RANK)
        spread = jnp.repeat(downward, 2, axis=0)
        downward = jnp.einsum("cvl,ckl->cvk", spread, matrices, precision=highest)
        if height - 1 <= LOCAL - 2:
            downward = downward + couplings[height - 1]
    rounded = lax.optimization_barrier(downward.astype(jnp.bfloat16))
    distant = jnp.einsum("tmk,tvk->tmv", leaf_basis.astype(jnp.float32), rounded.astype(jnp.float32), precision=highest)
    nearby = jnp.zeros(vectors.shape, jnp.float32)
    for column in range(NN):
        source = vectors[near_src[:, column]].astype(jnp.float32)
        nearby = nearby + jnp.einsum("tmn,tnv->tmv", near_blocks[:, :, column, :].astype(jnp.float32), source, precision=highest)
    return distant + nearby
```

```python
import functools

import jax
import jax.numpy as jnp
from jax import lax
from jax.experimental import pallas as pl
from jax.experimental.pallas import tpu as pltpu
from jax.sharding import PartitionSpec as P

MESH = pl.DeviceIdType.MESH
f32, bf16 = jnp.float32, jnp.bfloat16
NT = (((1,), (1,)), ((), ()))


def dot(a, b):
    return jnp.dot(a, b, preferred_element_type=f32)


def dot_nt(a, b):
    return lax.dot_general(a, b, NT, preferred_element_type=f32)


def parts(x):
    high = x.astype(bf16)
    return high, (x - high.astype(f32)).astype(bf16)


def twice(x):
    return jnp.concatenate([x, x], axis=1)


def kernel(
    tops, group, side,
    v_hbm, b_hbm, t_hbm, c_hbm, r_hbm, n_hbm, cs_hbm, rs_hbm, ns_hbm,
    out,
    vext, basis, transfer, couple, root, near, cs, rs, ns,
    x0, x1, lifted_rows, parts_in, tops_in, z_rows, q_high, q_low,
    in_sem, small_sem, halo_send, halo_recv, sum_send, sum_recv, top_send, top_recv, z_send, z_recv,
):
    leaf, grp = lax.axis_index("leaf"), lax.axis_index("grp")
    devices = tops * group
    me = leaf * group + grp

    def load(src, dst, sem):
        copy = pltpu.make_async_copy(src, dst, sem)
        copy.start()
        return copy

    v_copy = load(v_hbm, vext.at[pl.ds(2, 8)], in_sem.at[0])
    b_copy = load(b_hbm, basis, in_sem.at[1])
    t_copy = load(t_hbm, transfer, in_sem.at[2])
    cs_copy = load(cs_hbm, cs, small_sem.at[0])
    rs_copy = load(rs_hbm, rs, small_sem.at[1])
    ns_copy = load(ns_hbm, ns, small_sem.at[2])
    r_copy = load(r_hbm, root, in_sem.at[3])
    n_copies = [load(n_hbm.at[pl.ds(2 * i, 2)], near.at[pl.ds(2 * i, 2)], in_sem.at[5 + i]) for i in range(4)]
    c_copy = load(c_hbm, couple, in_sem.at[4])

    up, down = lax.rem(me + 1, devices), lax.rem(me + devices - 1, devices)
    up_id = (lax.div(up, group), lax.rem(up, group))
    down_id = (lax.div(down, group), lax.rem(down, group))
    barrier = pltpu.get_barrier_semaphore()

    def greet(device):
        pl.semaphore_signal(barrier, inc=1, device_id=device, device_id_type=MESH)

    def peer(o):
        return (leaf, lax.rem(grp + o, group))

    row_at, column = lax.div(leaf, side), lax.rem(leaf, side)

    def beside(o):
        return (row_at * side + lax.rem(column + o, side), grp)

    def over(o):
        return (lax.rem(row_at + o, tops // side) * side + column, grp)

    greet(up_id)
    greet(down_id)

    @pl.loop(1, group)
    def _(o):
        greet(peer(o))

    @pl.loop(1, side)
    def _(o):
        greet(beside(o))

    @pl.loop(1, tops // side)
    def _(o):
        greet(over(o))

    first = lax.broadcasted_iota(jnp.int32, (16, 128), 1) < 64
    first8 = lax.broadcasted_iota(jnp.int32, (8, 128), 1) < 64

    def split(x):
        high = x.astype(bf16).astype(f32)
        return jnp.where(first, high, x - high).astype(bf16)

    v_copy.wait()
    b_copy.wait()
    level = []
    for t in range(8):
        b = basis[t]
        x = split(dot_nt(vext[2 + t], jnp.concatenate([b, b], axis=0)))
        x0[3 + t] = x
        level.append(x)

    t_copy.wait()
    e_high, e_low = [], []
    for i in range(15):
        high, low = parts(twice(transfer[i]))
        e_high.append(high)
        e_low.append(low)

    def lift(x, i):
        weights = jnp.concatenate([e_high[i], e_high[i], e_low[i], e_low[i]], axis=0)
        return dot(twice(x), weights)

    offset = 0
    for height in range(1, 4):
        clusters = 16 >> height
        above = []
        for q in range(clusters // 2):
            x = split(lift(level[2 * q], offset + 2 * q) + lift(level[2 * q + 1], offset + 2 * q + 1))
            if height == 1:
                x1[3 + q] = x
            above.append(x)
        offset += clusters
        level = above
    top = lift(level[0], 14)
    packed = jnp.where(first8, top[0:8], top[8:16])
    lifted_rows[...] = packed.reshape(8, 1, 128)

    pl.semaphore_wait(barrier, 2 + (group - 1) + (side - 1) + (tops // side - 1))

    @pl.loop(1, group)
    def _(o):
        pltpu.make_async_remote_copy(
            lifted_rows.at[lax.rem(grp + o, group)], parts_in.at[o], sum_send, sum_recv, peer(o), MESH
        ).start()

    halos = []

    def halo(src, dst, n, device):
        copy = pltpu.make_async_remote_copy(src, dst, halo_send.at[n], halo_recv.at[n], device, MESH)
        copy.start()
        halos.append(copy)

    halo(vext.at[pl.ds(8, 2)], vext.at[pl.ds(0, 2)], 0, up_id)
    halo(vext.at[pl.ds(2, 2)], vext.at[pl.ds(10, 2)], 1, down_id)
    halo(x0.at[pl.ds(8, 3)], x0.at[pl.ds(0, 3)], 2, up_id)
    halo(x0.at[pl.ds(3, 3)], x0.at[pl.ds(11, 3)], 3, down_id)
    halo(x1.at[pl.ds(4, 3)], x1.at[pl.ds(0, 3)], 4, up_id)
    halo(x1.at[pl.ds(3, 3)], x1.at[pl.ds(7, 3)], 5, down_id)

    def chain(i, right):
        high, low = right
        e_h, e_l = e_high[i], e_low[i]
        left = jnp.where(lax.broadcasted_iota(jnp.int32, (64, 128), 1) < 64, e_h, e_l)
        return dot(twice(left), jnp.concatenate([high, high, low, low], axis=0))

    q3 = (e_high[14], e_low[14])
    q2 = [parts(chain(12 + i, q3)) for i in range(2)]
    q1 = [parts(chain(8 + i, q2[i // 2])) for i in range(4)]
    for c in range(8):
        high, low = parts(chain(c, q1[c // 2]))
        q_high[pl.ds(64 * c, 64)] = high
        q_low[pl.ds(64 * c, 64)] = low

    pltpu.make_async_copy(parts_in.at[pl.ds(1, group - 1)], parts_in.at[pl.ds(1, group - 1)], sum_recv).wait()
    total = lifted_rows[grp]
    for o in range(1, group):
        total = total + parts_in[o]
    tops_in[leaf] = total

    @pl.loop(1, side)
    def _(o):
        pltpu.make_async_remote_copy(
            tops_in.at[leaf], tops_in.at[leaf], top_send.at[0], top_recv.at[0], beside(o), MESH
        ).start()

    others = tops_in.at[pl.ds(0, side - 1)]
    pltpu.make_async_copy(others, others, top_recv.at[0]).wait()
    block = tops_in.at[pl.ds(row_at * side, side)]

    @pl.loop(1, tops // side)
    def _(o):
        pltpu.make_async_remote_copy(block, block, top_send.at[1], top_recv.at[1], over(o), MESH).start()

    r_copy.wait()
    diagonal = []
    for j in range(4):
        m = root[j]
        zero = jnp.zeros_like(m)
        diagonal.append(
            parts(jnp.concatenate([jnp.concatenate([m, zero], axis=1), jnp.concatenate([zero, m], axis=1)], axis=0))
        )
    rs_copy.wait()
    ns_copy.wait()
    cs_copy.wait()
    for copy in halos:
        copy.wait_recv()
    for copy in n_copies:
        copy.wait()
    for t in range(8):
        total = dot_nt(vext[2 + t], near[t, 0])
        for e in range(1, 3):
            place = jnp.minimum(jnp.bitwise_and(ns[e, t] - 8 * me + 2, 8 * devices - 1), 11)
            total = total + dot_nt(vext[place], near[t, e])
        out[t] = total

    c_copy.wait()

    def coupling(x, row, base, cycle):
        total = None
        for j in range(3):
            place = jnp.minimum(jnp.bitwise_and(cs[j, 0, row] - base + 3, cycle - 1), x.shape[0] - 1)
            high, low = parts(couple[3 * row + j])
            term = dot(twice(x[place]), jnp.concatenate([high, high, low, low], axis=0))
            total = term if total is None else total + term
        return total

    pairs = []
    for q in range(4):
        y1 = split(twice(coupling(x1, 8 + q, 4 * me, 4 * devices)))
        weights = jnp.concatenate(
            [
                jnp.concatenate([e_high[2 * q], e_low[2 * q]], axis=1),
                jnp.concatenate([e_high[2 * q + 1], e_low[2 * q + 1]], axis=1),
            ],
            axis=0,
        )
        y0 = [coupling(x0, 2 * q + i, 8 * me, 8 * devices) for i in range(2)]
        pairs.append(dot_nt(twice(y1), weights) + jnp.concatenate(y0, axis=1))
    base = jnp.concatenate(pairs, axis=1)

    others = tops_in.at[pl.ds(0, tops - side)]
    pltpu.make_async_copy(others, others, top_recv.at[1]).wait()
    row = None
    for j in range(4):
        slot = jnp.bitwise_and(rs[0, j], tops - 1)
        g_high, g_low = parts(tops_in[slot])
        r_high, r_low = diagonal[j]
        term = dot(g_high, r_high) + dot(g_low, r_high) + dot(g_high, r_low)
        row = term if row is None else row + term
    z_rows[grp] = row

    @pl.loop(1, group)
    def _(o):
        pltpu.make_async_remote_copy(z_rows.at[grp], z_rows.at[grp], z_send, z_recv.at[grp], peer(o), MESH).start()

    @pl.loop(1, group)
    def _(o):
        other = lax.rem(grp + o, group)
        pltpu.make_async_remote_copy(
            z_rows.at[other], z_rows.at[other], z_send, z_recv.at[other], peer(o), MESH
        ).wait_recv()

    z = z_rows[...].reshape(8, 128)
    zero = jnp.zeros_like(z)
    z = jnp.concatenate([jnp.where(first8, z, zero), jnp.where(first8, zero, z)], axis=0)
    z_high, z_low = parts(z)
    low_q = q_low[...]
    high_q = q_high[...]
    w = dot_nt(z_high, high_q) + dot_nt(z_low, high_q) + dot_nt(z_high, low_q) + base
    w = w.astype(bf16)
    nothing = jnp.zeros((16, 128), bf16)
    for q in range(4):
        pair = w[:, 128 * q : 128 * (q + 1)]
        left = jnp.concatenate([jnp.where(first, pair, nothing), jnp.where(first, nothing, pair)], axis=0)
        product = dot(left, basis[2 * q : 2 * q + 2].reshape(128, 256))
        out[2 * q] = out[2 * q] + product[0:16]
        out[2 * q + 1] = out[2 * q + 1] + product[16:32]

    for copy in halos:
        copy.wait_send()
    sent = parts_in.at[pl.ds(1, group - 1)]
    pltpu.make_async_copy(sent, sent, sum_send).wait()
    pltpu.make_async_copy(sent, sent, z_send).wait()
    sent = tops_in.at[pl.ds(0, side - 1)]
    pltpu.make_async_copy(sent, sent, top_send.at[0]).wait()
    sent = tops_in.at[pl.ds(0, tops - side)]
    pltpu.make_async_copy(sent, sent, top_send.at[1]).wait()


def solution(mesh):
    tops, group = mesh.shape["leaf"], mesh.shape["grp"]

    def body(vectors, leaf_basis, transfer, couple_src, couple_mat, root_src, root_mat, near_src, near_blocks):
        args = (
            vectors.transpose(0, 2, 1),
            leaf_basis.transpose(0, 2, 1),
            transfer.reshape(15, 64, 64),
            couple_mat.reshape(36, 64, 64),
            root_mat.reshape(4, 64, 64),
            near_blocks.transpose(0, 2, 1, 3),
            couple_src.transpose(2, 0, 1),
            root_src,
            near_src.transpose(1, 0),
        )
        hbm = pl.BlockSpec(memory_space=pltpu.HBM)
        dma = pltpu.SemaphoreType.DMA
        result = pl.pallas_call(
            functools.partial(kernel, tops, group, 8),
            out_shape=pltpu.VMEM((8, 16, 256), f32),
            in_specs=[hbm] * 9,
            out_specs=pl.BlockSpec(memory_space=pltpu.VMEM),
            scratch_shapes=[
                pltpu.VMEM((12, 16, 256), bf16),
                pltpu.VMEM((8, 64, 256), bf16),
                pltpu.VMEM((15, 64, 64), f32),
                pltpu.VMEM((36, 64, 64), f32),
                pltpu.VMEM((4, 64, 64), f32),
                pltpu.VMEM((8, 3, 256, 256), bf16),
                pltpu.SMEM((3, 1, 12), jnp.int32),
                pltpu.SMEM((1, 4), jnp.int32),
                pltpu.SMEM((3, 8), jnp.int32),
                pltpu.VMEM((14, 16, 128), bf16),
                pltpu.VMEM((10, 16, 128), bf16),
                pltpu.VMEM((8, 1, 128), f32),
                pltpu.VMEM((8, 1, 128), f32),
                pltpu.VMEM((tops, 1, 128), f32),
                pltpu.VMEM((8, 1, 128), f32),
                pltpu.VMEM((512, 128), bf16),
                pltpu.VMEM((512, 128), bf16),
                dma((9,)),
                dma((3,)),
                dma((6,)),
                dma((6,)),
                dma,
                dma,
                dma((2,)),
                dma((2,)),
                dma,
                dma((8,)),
            ],
            compiler_params=pltpu.CompilerParams(
                collective_id=0, has_side_effects=True, vmem_limit_bytes=32 * 1024 * 1024
            ),
            name="h2",
        )(*(pltpu.with_memory_space_constraint(a, pltpu.HBM) for a in args))
        return result.transpose(0, 2, 1)

    both = ("leaf", "grp")
    in_specs = (
        P(both, None, None),
        P(both, None, None),
        P(both, None, None, None),
        P(both, None, None),
        P(both, None, None, None, None),
        P("leaf", None),
        P("leaf", None, None, None),
        P(both, None),
        P(both, None, None, None),
    )
    return jax.shard_map(body, mesh=mesh, in_specs=in_specs, out_specs=P(both, None, None), check_vma=False)
```

```python
import functools

import jax
import jax.numpy as jnp
from jax import lax
from jax.experimental import pallas as pl
from jax.experimental.pallas import tpu as pltpu
from jax.sharding import PartitionSpec as P

MESH = pl.DeviceIdType.MESH
f32, bf16 = jnp.float32, jnp.bfloat16
RELAY = 5
NT = (((1,), (1,)), ((), ()))


def dot(a, b):
    return jnp.dot(a, b, preferred_element_type=f32)


def dot_nt(a, b):
    return lax.dot_general(a, b, NT, preferred_element_type=f32)


def parts(x):
    high = x.astype(bf16)
    return high, (x - high.astype(f32)).astype(bf16)


def twice(x):
    return jnp.concatenate([x, x], axis=1)


def kernel(
    tops, group, side,
    v_hbm, b_hbm, t_hbm, c_hbm, r_hbm, n_hbm, cs_hbm, rs_hbm, ns_hbm,
    out,
    vext, basis, transfer, couple, root, near, cs, rs, ns,
    x0, x1, lifted_rows, parts_in, tops_in, z_rows, q_high, q_low, stack,
    in_sem, small_sem, halo_send, halo_recv, sum_send, sum_recv, own_send, relay_send, top_recv, z_send, z_recv,
):
    leaf, grp = lax.axis_index("leaf"), lax.axis_index("grp")
    devices = tops * group
    me = leaf * group + grp

    def load(src, dst, sem):
        copy = pltpu.make_async_copy(src, dst, sem)
        copy.start()
        return copy

    v_copy = load(v_hbm, vext.at[pl.ds(2, 8)], in_sem.at[0])
    b_copy = load(b_hbm, basis, in_sem.at[1])
    t_copy = load(t_hbm, transfer, in_sem.at[2])
    cs_copy = load(cs_hbm, cs, small_sem.at[0])
    rs_copy = load(rs_hbm, rs, small_sem.at[1])
    ns_copy = load(ns_hbm, ns, small_sem.at[2])

    up, down = lax.rem(me + 1, devices), lax.rem(me + devices - 1, devices)
    up_id = (lax.div(up, group), lax.rem(up, group))
    down_id = (lax.div(down, group), lax.rem(down, group))
    barrier = pltpu.get_barrier_semaphore()

    def greet(device):
        pl.semaphore_signal(barrier, inc=1, device_id=device, device_id_type=MESH)

    def turn(i, n):
        return jnp.where(i >= n, i - n, i)

    def peer(o):
        return (leaf, turn(grp + o, group))

    row_at, column = lax.div(leaf, side), lax.rem(leaf, side)
    planes = tops // side
    plane = side * group
    place_in = column * group + grp

    def at(z):
        return (z * side + column, grp)

    def sends(z, t):
        return (z != t) & ((t <= RELAY) | ((z != RELAY - 1) & (z != RELAY - 2)))

    is_relayed = (row_at == RELAY - 1) | (row_at == RELAY - 2)
    targets = planes - 1 - jnp.where(is_relayed, planes - 1 - RELAY, 0)

    def through_plane(act):
        @pl.loop(0, side - 1)
        def _(k):
            o = turn(k + side // 2, side)
            other = row_at * side + turn(column + jnp.where(k + side // 2 >= side, o + 1, o), side)
            for g in range(group):
                act((other, g), g)

        for o in range(1, group):
            device = peer(o)
            act(device, device[1])

    greet(up_id)
    greet(down_id)
    through_plane(lambda device, g: greet(device))

    for z in range(planes):
        pl.when(sends(z, row_at))(functools.partial(lambda z: greet(at(z)), z))

    first = lax.broadcasted_iota(jnp.int32, (16, 128), 1) < 64
    first8 = lax.broadcasted_iota(jnp.int32, (8, 128), 1) < 64

    def split(x):
        high = x.astype(bf16).astype(f32)
        return jnp.where(first, high, x - high).astype(bf16)

    v_copy.wait()
    b_copy.wait()
    level = []
    for t in range(8):
        b = basis[t]
        x = split(dot_nt(vext[2 + t], jnp.concatenate([b, b], axis=0)))
        x0[3 + t] = x
        level.append(x)

    t_copy.wait()
    r_copy = load(r_hbm, root, in_sem.at[3])
    n_copies = [load(n_hbm.at[pl.ds(2 * i, 2)], near.at[pl.ds(2 * i, 2)], in_sem.at[5 + i]) for i in range(4)]
    c_copy = load(c_hbm, couple, in_sem.at[4])
    e_high, e_low = [], []
    for i in range(15):
        high, low = parts(twice(transfer[i]))
        e_high.append(high)
        e_low.append(low)

    def lift(x, i):
        weights = jnp.concatenate([e_high[i], e_high[i], e_low[i], e_low[i]], axis=0)
        return dot(twice(x), weights)

    offset = 0
    for height in range(1, 4):
        clusters = 16 >> height
        above = []
        for q in range(clusters // 2):
            x = split(lift(level[2 * q], offset + 2 * q) + lift(level[2 * q + 1], offset + 2 * q + 1))
            if height == 1:
                x1[3 + q] = x
            above.append(x)
        offset += clusters
        level = above
    top = lift(level[0], 14)
    packed = jnp.where(first8, top[0:8], top[8:16])
    lifted_rows[...] = packed.reshape(8, 1, 128)

    pl.semaphore_wait(barrier, 2 + (plane - 1) + targets)

    def hand_out(device, g):
        pltpu.make_async_remote_copy(
            lifted_rows.at[g], parts_in.at[place_in], sum_send, sum_recv, device, MESH
        ).start()

    through_plane(hand_out)
    parts_in[place_in] = lifted_rows[grp]

    halos = []

    def halo(src, dst, n, device):
        copy = pltpu.make_async_remote_copy(src, dst, halo_send.at[n], halo_recv.at[n], device, MESH)
        copy.start()
        halos.append(copy)

    halo(vext.at[pl.ds(8, 2)], vext.at[pl.ds(0, 2)], 0, up_id)
    halo(vext.at[pl.ds(2, 2)], vext.at[pl.ds(10, 2)], 1, down_id)
    halo(x0.at[pl.ds(8, 3)], x0.at[pl.ds(0, 3)], 2, up_id)
    halo(x0.at[pl.ds(3, 3)], x0.at[pl.ds(11, 3)], 3, down_id)
    halo(x1.at[pl.ds(4, 3)], x1.at[pl.ds(0, 3)], 4, up_id)
    halo(x1.at[pl.ds(3, 3)], x1.at[pl.ds(7, 3)], 5, down_id)

    def chain(i, right):
        high, low = right
        e_h, e_l = e_high[i], e_low[i]
        left = jnp.where(lax.broadcasted_iota(jnp.int32, (64, 128), 1) < 64, e_h, e_l)
        return dot(twice(left), jnp.concatenate([high, high, low, low], axis=0))

    q3 = (e_high[14], e_low[14])
    q2 = [parts(chain(12 + i, q3)) for i in range(2)]
    q1 = [parts(chain(8 + i, q2[i // 2])) for i in range(4)]
    for c in range(8):
        high, low = parts(chain(c, q1[c // 2]))
        q_high[pl.ds(64 * c, 64)] = high
        q_low[pl.ds(64 * c, 64)] = low

    r_copy.wait()
    highs, lows = [], []
    for j in range(4):
        m = root[j]
        zero = jnp.zeros_like(m)
        diagonal = jnp.concatenate([jnp.concatenate([m, zero], axis=1), jnp.concatenate([zero, m], axis=1)], axis=0)
        high, low = parts(diagonal)
        highs.append(high)
        lows.append(low)
    stack[...] = jnp.concatenate(highs + highs + lows, axis=0)
    for i in range(4):
        n_copies[i].wait()
        for t in range(2 * i, 2 * i + 2):
            out[t] = dot_nt(vext[2 + t], near[t, 0])

    others = parts_in.at[pl.ds(0, plane - 1)]
    pltpu.make_async_copy(others, others, sum_recv).wait()
    sums = parts_in[...].reshape(side, group, 128).sum(axis=1)
    tops_in[pl.ds(row_at * side, side)] = sums.reshape(side, 1, 128)

    def block(z):
        return tops_in.at[pl.ds(z * side, side)]

    def pass_on(z, send, target):
        return pltpu.make_async_remote_copy(block(z), block(z), send, top_recv.at[z], at(target), MESH)

    def arrive(z):
        pltpu.make_async_copy(block(z), block(z), top_recv.at[z]).wait()

    def each_target(act):
        for z in range(planes):
            pl.when(sends(row_at, z))(functools.partial(act, z))

    each_target(lambda z: pass_on(row_at, own_send.at[z], z).start())

    @pl.when(row_at == RELAY)
    def _():
        for i in range(2):
            arrive(RELAY - 1 - i)
            for z in range(RELAY + 1, planes):
                pass_on(RELAY - 1 - i, relay_send.at[i, z], z).start()

    rs_copy.wait()
    ns_copy.wait()
    cs_copy.wait()
    for copy in halos:
        copy.wait_recv()
    for t in range(8):
        total = out[t]
        for e in range(1, 3):
            place = jnp.minimum(jnp.bitwise_and(ns[e, t] - 8 * me + 2, 8 * devices - 1), 11)
            total = total + dot_nt(vext[place], near[t, e])
        out[t] = total

    c_copy.wait()

    def coupling(x, row, base, cycle):
        total = None
        for j in range(3):
            place = jnp.minimum(jnp.bitwise_and(cs[j, 0, row] - base + 3, cycle - 1), x.shape[0] - 1)
            high, low = parts(couple[3 * row + j])
            term = dot(twice(x[place]), jnp.concatenate([high, high, low, low], axis=0))
            total = term if total is None else total + term
        return total

    pairs = []
    for q in range(4):
        y1 = split(twice(coupling(x1, 8 + q, 4 * me, 4 * devices)))
        weights = jnp.concatenate(
            [
                jnp.concatenate([e_high[2 * q], e_low[2 * q]], axis=1),
                jnp.concatenate([e_high[2 * q + 1], e_low[2 * q + 1]], axis=1),
            ],
            axis=0,
        )
        y0 = [coupling(x0, 2 * q + i, 8 * me, 8 * devices) for i in range(2)]
        pairs.append(dot_nt(twice(y1), weights) + jnp.concatenate(y0, axis=1))
    base = jnp.concatenate(pairs, axis=1)

    for z in range(planes):
        expected = row_at != z
        if z in (RELAY - 1, RELAY - 2):
            expected = expected & (row_at != RELAY)
        pl.when(expected)(functools.partial(arrive, z))

    g = jnp.concatenate([tops_in[jnp.bitwise_and(rs[0, j], tops - 1)] for j in range(4)], axis=1)
    high, low = parts(g)
    row = dot(jnp.concatenate([high, low, high], axis=1), stack[...])
    z_rows[grp] = row

    for o in range(1, group):
        pltpu.make_async_remote_copy(z_rows.at[grp], z_rows.at[grp], z_send, z_recv, peer(o), MESH).start()
    others = z_rows.at[pl.ds(0, group - 1)]
    pltpu.make_async_copy(others, others, z_recv).wait()

    z = z_rows[...].reshape(8, 128)
    zero = jnp.zeros_like(z)
    z = jnp.concatenate([jnp.where(first8, z, zero), jnp.where(first8, zero, z)], axis=0)
    z_high, z_low = parts(z)
    low_q = q_low[...]
    high_q = q_high[...]
    product = dot_nt(jnp.concatenate([z_high, z_low], axis=0), high_q)
    w = product[0:16] + product[16:32] + dot_nt(z_high, low_q) + base
    w = w.astype(bf16)
    nothing = jnp.zeros((16, 128), bf16)
    for q in range(4):
        pair = w[:, 128 * q : 128 * (q + 1)]
        left = jnp.concatenate([jnp.where(first, pair, nothing), jnp.where(first, nothing, pair)], axis=0)
        product = dot(left, basis[2 * q : 2 * q + 2].reshape(128, 256))
        out[2 * q] = out[2 * q] + product[0:16]
        out[2 * q + 1] = out[2 * q + 1] + product[16:32]

    for copy in halos:
        copy.wait_send()
    sent = parts_in.at[pl.ds(0, plane - 1)]
    pltpu.make_async_copy(sent, sent, sum_send).wait()

    each_target(lambda z: pass_on(row_at, own_send.at[z], z).wait_send())

    @pl.when(row_at == RELAY)
    def _():
        for i in range(2):
            for z in range(RELAY + 1, planes):
                pass_on(RELAY - 1 - i, relay_send.at[i, z], z).wait_send()

    sent = parts_in.at[pl.ds(0, group - 1)]
    pltpu.make_async_copy(sent, sent, z_send).wait()


def solution(mesh):
    tops, group = mesh.shape["leaf"], mesh.shape["grp"]

    def body(vectors, leaf_basis, transfer, couple_src, couple_mat, root_src, root_mat, near_src, near_blocks):
        args = (
            vectors.transpose(0, 2, 1),
            leaf_basis.transpose(0, 2, 1),
            transfer.reshape(15, 64, 64),
            couple_mat.reshape(36, 64, 64),
            root_mat.reshape(4, 64, 64),
            near_blocks.transpose(0, 2, 1, 3),
            couple_src.transpose(2, 0, 1),
            root_src,
            near_src.transpose(1, 0),
        )
        hbm = pl.BlockSpec(memory_space=pltpu.HBM)
        dma = pltpu.SemaphoreType.DMA
        result = pl.pallas_call(
            functools.partial(kernel, tops, group, 8),
            out_shape=pltpu.VMEM((8, 16, 256), f32),
            in_specs=[hbm] * 9,
            out_specs=pl.BlockSpec(memory_space=pltpu.VMEM),
            scratch_shapes=[
                pltpu.VMEM((12, 16, 256), bf16),
                pltpu.VMEM((8, 64, 256), bf16),
                pltpu.VMEM((15, 64, 64), f32),
                pltpu.VMEM((36, 64, 64), f32),
                pltpu.VMEM((4, 64, 64), f32),
                pltpu.VMEM((8, 3, 256, 256), bf16),
                pltpu.SMEM((3, 1, 12), jnp.int32),
                pltpu.SMEM((1, 4), jnp.int32),
                pltpu.SMEM((3, 8), jnp.int32),
                pltpu.VMEM((14, 16, 128), bf16),
                pltpu.VMEM((10, 16, 128), bf16),
                pltpu.VMEM((8, 1, 128), f32),
                pltpu.VMEM((64, 1, 128), f32),
                pltpu.VMEM((tops, 1, 128), f32),
                pltpu.VMEM((8, 1, 128), f32),
                pltpu.VMEM((512, 128), bf16),
                pltpu.VMEM((512, 128), bf16),
                pltpu.VMEM((1536, 128), bf16),
                dma((9,)),
                dma((3,)),
                dma((6,)),
                dma((6,)),
                dma,
                dma,
                dma((8,)),
                dma((2, 8)),
                dma((8,)),
                dma,
                dma,
            ],
            compiler_params=pltpu.CompilerParams(
                collective_id=0, has_side_effects=True, vmem_limit_bytes=32 * 1024 * 1024
            ),
            name="h2",
        )(*(pltpu.with_memory_space_constraint(a, pltpu.HBM) for a in args))
        return result.transpose(0, 2, 1)

    both = ("leaf", "grp")
    in_specs = (
        P(both, None, None),
        P(both, None, None),
        P(both, None, None, None),
        P(both, None, None),
        P(both, None, None, None, None),
        P("leaf", None),
        P("leaf", None, None, None),
        P(both, None),
        P(both, None, None, None),
    )
    return jax.shard_map(body, mesh=mesh, in_specs=in_specs, out_specs=P(both, None, None), check_vma=False)
```

```python
import functools

import jax
import jax.numpy as jnp
from jax import lax
from jax.experimental import pallas as pl
from jax.experimental.pallas import tpu as pltpu
from jax.sharding import PartitionSpec as P

MESH = pl.DeviceIdType.MESH
f32, bf16 = jnp.float32, jnp.bfloat16
RELAY = 5
OWNERS = 4
NT = (((1,), (1,)), ((), ()))


def dot(a, b):
    return jnp.dot(a, b, preferred_element_type=f32)


def dot_nt(a, b):
    return lax.dot_general(a, b, NT, preferred_element_type=f32)


def parts(x):
    high = x.astype(bf16)
    return high, (x - high.astype(f32)).astype(bf16)


def twice(x):
    return jnp.concatenate([x, x], axis=1)


def kernel(
    tops, group, side,
    v_hbm, b_hbm, t_hbm, c_hbm, r_hbm, n_hbm, cs_hbm, rs_hbm, ns_hbm,
    out,
    vext, basis, transfer, couple, root, near, cs, rs, ns,
    x0, x1, lifted_rows, parts_in, tops_in, z_rows, q_high, q_low, stack,
    in_sem, small_sem, halo_send, halo_recv, sum_send, sum_recv, own_send, relay_send, top_recv, z_send, z_recv,
):
    leaf, grp = lax.axis_index("leaf"), lax.axis_index("grp")
    devices = tops * group
    me = leaf * group + grp

    def load(src, dst, sem):
        copy = pltpu.make_async_copy(src, dst, sem)
        copy.start()
        return copy

    v_copy = load(v_hbm, vext.at[pl.ds(2, 8)], in_sem.at[0])
    b_copy = load(b_hbm, basis, in_sem.at[1])
    t_copy = load(t_hbm, transfer, in_sem.at[2])

    up, down = lax.rem(me + 1, devices), lax.rem(me + devices - 1, devices)
    up_id = (lax.div(up, group), lax.rem(up, group))
    down_id = (lax.div(down, group), lax.rem(down, group))
    barrier = pltpu.get_barrier_semaphore()

    def greet(device):
        pl.semaphore_signal(barrier, inc=1, device_id=device, device_id_type=MESH)

    def turn(i, n):
        return jnp.where(i >= n, i - n, i)

    def peer(o):
        return (leaf, turn(grp + o, group))

    row_at, column = lax.div(leaf, side), lax.rem(leaf, side)
    planes = tops // side
    plane = side * group
    place_in = column * group + grp

    def at(z):
        return (z * side + column, grp)

    def sends(z, t):
        return (z != t) & ((t <= RELAY) | ((z != RELAY - 1) & (z != RELAY - 2)))

    is_relayed = (row_at == RELAY - 1) | (row_at == RELAY - 2)
    targets = planes - 1 - jnp.where(is_relayed, planes - 1 - RELAY, 0)

    owner = grp < OWNERS

    def through_columns(act, count):
        @pl.loop(0, side - 1)
        def _(k):
            o = turn(k + side // 2, side)
            other = row_at * side + turn(column + jnp.where(k + side // 2 >= side, o + 1, o), side)
            for g in range(count):
                act((other, g), g)

    def owners_here(act):
        for g in range(OWNERS):
            pl.when(grp != g)(functools.partial(act, (leaf, g), g))

    @pl.when(owner)
    def _():
        through_columns(lambda device, g: greet(device), group)
        for o in range(1, group):
            greet(peer(o))
        for z in range(planes):
            pl.when(sends(z, row_at))(functools.partial(lambda z: greet(at(z)), z))

    @pl.when(grp >= OWNERS)
    def _():
        for g in range(OWNERS):
            greet((leaf, g))

    greet(up_id)
    greet(down_id)

    first = lax.broadcasted_iota(jnp.int32, (16, 128), 1) < 64
    first8 = lax.broadcasted_iota(jnp.int32, (8, 128), 1) < 64

    def split(x):
        high = x.astype(bf16).astype(f32)
        return jnp.where(first, high, x - high).astype(bf16)

    v_copy.wait()
    b_copy.wait()
    level = []
    for t in range(8):
        b = basis[t]
        x = split(dot_nt(vext[2 + t], jnp.concatenate([b, b], axis=0)))
        x0[3 + t] = x
        level.append(x)

    t_copy.wait()
    cs_copy = load(cs_hbm, cs, small_sem.at[0])
    rs_copy = load(rs_hbm, rs, small_sem.at[1])
    ns_copy = load(ns_hbm, ns, small_sem.at[2])
    r_copy = load(r_hbm, root, in_sem.at[3])
    n_copies = [load(n_hbm.at[pl.ds(2 * i, 2)], near.at[pl.ds(2 * i, 2)], in_sem.at[5 + i]) for i in range(4)]
    c_copy = load(c_hbm, couple, in_sem.at[4])
    e_high, e_low = [], []
    for i in range(15):
        high, low = parts(twice(transfer[i]))
        e_high.append(high)
        e_low.append(low)

    def lift(x, i):
        weights = jnp.concatenate([e_high[i], e_high[i], e_low[i], e_low[i]], axis=0)
        return dot(twice(x), weights)

    def chain(i, right):
        high, low = right
        e_h, e_l = e_high[i], e_low[i]
        left = jnp.where(lax.broadcasted_iota(jnp.int32, (64, 128), 1) < 64, e_h, e_l)
        return dot(twice(left), jnp.concatenate([high, high, low, low], axis=0))

    q2 = [parts(chain(12 + i, (e_high[14], e_low[14]))) for i in range(2)]
    offset = 0
    for height in range(1, 3):
        clusters = 16 >> height
        above = []
        for q in range(clusters // 2):
            x = split(lift(level[2 * q], offset + 2 * q) + lift(level[2 * q + 1], offset + 2 * q + 1))
            if height == 1:
                x1[3 + q] = x
            above.append(x)
        offset += clusters
        level = above
    top = None
    for x, (high, low) in zip(level, q2):
        term = dot(twice(x), jnp.concatenate([high, high, low, low], axis=0))
        top = term if top is None else top + term
    packed = jnp.where(first8, top[0:8], top[8:16])
    for i in range(4):
        lifted_rows[i] = packed[2 * i : 2 * i + 2]

    pl.semaphore_wait(
        barrier, 2 + side * OWNERS + jnp.where(owner, group - OWNERS - 1 + targets, 0)
    )

    def hand_out(device, g):
        pltpu.make_async_remote_copy(
            lifted_rows.at[g], parts_in.at[place_in], sum_send, sum_recv, device, MESH
        ).start()

    through_columns(hand_out, OWNERS)
    owners_here(hand_out)

    @pl.when(owner)
    def _():
        parts_in[place_in] = lifted_rows[grp]

    halos = []

    def halo(src, dst, n, device):
        copy = pltpu.make_async_remote_copy(src, dst, halo_send.at[n], halo_recv.at[n], device, MESH)
        copy.start()
        halos.append(copy)

    halo(vext.at[pl.ds(8, 2)], vext.at[pl.ds(0, 2)], 0, up_id)
    halo(vext.at[pl.ds(2, 2)], vext.at[pl.ds(10, 2)], 1, down_id)
    halo(x0.at[pl.ds(8, 3)], x0.at[pl.ds(0, 3)], 2, up_id)
    halo(x0.at[pl.ds(3, 3)], x0.at[pl.ds(11, 3)], 3, down_id)
    halo(x1.at[pl.ds(4, 3)], x1.at[pl.ds(0, 3)], 4, up_id)
    halo(x1.at[pl.ds(3, 3)], x1.at[pl.ds(7, 3)], 5, down_id)

    q1 = [parts(chain(8 + i, q2[i // 2])) for i in range(4)]
    for c in range(8):
        high, low = parts(chain(c, q1[c // 2]))
        q_high[pl.ds(64 * c, 64)] = high
        q_low[pl.ds(64 * c, 64)] = low

    r_copy.wait()
    highs, lows = [], []
    for j in range(4):
        m = root[j]
        zero = jnp.zeros_like(m)
        diagonal = jnp.concatenate([jnp.concatenate([m, zero], axis=1), jnp.concatenate([zero, m], axis=1)], axis=0)
        high, low = parts(diagonal)
        highs.append(high)
        lows.append(low)
    stack[...] = jnp.concatenate(highs + highs + lows, axis=0)
    for i in range(4):
        n_copies[i].wait()
        for t in range(2 * i, 2 * i + 2):
            out[t] = dot_nt(vext[2 + t], near[t, 0])

    def block(z):
        return tops_in.at[pl.ds(z * side, side)]

    def pass_on(z, send, target):
        return pltpu.make_async_remote_copy(block(z), block(z), send, top_recv.at[z], at(target), MESH)

    def arrive(z):
        pltpu.make_async_copy(block(z), block(z), top_recv.at[z]).wait()

    def each_target(act):
        for z in range(planes):
            pl.when(sends(row_at, z))(functools.partial(act, z))

    @pl.when(owner)
    def _():
        others = parts_in.at[pl.ds(0, plane - 1)]
        pltpu.make_async_copy(others, others, sum_recv).wait()
        tops_in[pl.ds(row_at * side, side)] = parts_in[...].reshape(side, group, 2, 128).sum(axis=1)
        each_target(lambda z: pass_on(row_at, own_send.at[z], z).start())

    @pl.when(owner & (row_at == RELAY))
    def _():
        for i in range(2):
            arrive(RELAY - 1 - i)
            for z in range(RELAY + 1, planes):
                pass_on(RELAY - 1 - i, relay_send.at[i, z], z).start()

    rs_copy.wait()
    ns_copy.wait()
    cs_copy.wait()
    for copy in halos:
        copy.wait_recv()
    for t in range(8):
        total = out[t]
        for e in range(1, 3):
            place = jnp.minimum(jnp.bitwise_and(ns[e, t] - 8 * me + 2, 8 * devices - 1), 11)
            total = total + dot_nt(vext[place], near[t, e])
        out[t] = total

    c_copy.wait()

    def coupling(x, row, base, cycle):
        total = None
        for j in range(3):
            place = jnp.minimum(jnp.bitwise_and(cs[j, 0, row] - base + 3, cycle - 1), x.shape[0] - 1)
            high, low = parts(couple[3 * row + j])
            term = dot(twice(x[place]), jnp.concatenate([high, high, low, low], axis=0))
            total = term if total is None else total + term
        return total

    pairs = []
    for q in range(4):
        y1 = split(twice(coupling(x1, 8 + q, 4 * me, 4 * devices)))
        weights = jnp.concatenate(
            [
                jnp.concatenate([e_high[2 * q], e_low[2 * q]], axis=1),
                jnp.concatenate([e_high[2 * q + 1], e_low[2 * q + 1]], axis=1),
            ],
            axis=0,
        )
        y0 = [coupling(x0, 2 * q + i, 8 * me, 8 * devices) for i in range(2)]
        pairs.append(dot_nt(twice(y1), weights) + jnp.concatenate(y0, axis=1))
    base = jnp.concatenate(pairs, axis=1)

    @pl.when(owner)
    def _():
        for z in range(planes):
            expected = row_at != z
            if z in (RELAY - 1, RELAY - 2):
                expected = expected & (row_at != RELAY)
            pl.when(expected)(functools.partial(arrive, z))
        g = jnp.concatenate([tops_in[jnp.bitwise_and(rs[0, j], tops - 1)] for j in range(4)], axis=1)
        high, low = parts(g)
        z_rows[grp] = dot(jnp.concatenate([high, low, high], axis=1), stack[...])
        for o in range(1, group):
            pltpu.make_async_remote_copy(z_rows.at[grp], z_rows.at[grp], z_send, z_recv, peer(o), MESH).start()
        others = z_rows.at[pl.ds(0, OWNERS - 1)]
        pltpu.make_async_copy(others, others, z_recv).wait()

    @pl.when(grp >= OWNERS)
    def _():
        pltpu.make_async_copy(z_rows, z_rows, z_recv).wait()

    z = jnp.concatenate([z_rows[i] for i in range(4)], axis=0)
    zero = jnp.zeros_like(z)
    z = jnp.concatenate([jnp.where(first8, z, zero), jnp.where(first8, zero, z)], axis=0)
    z_high, z_low = parts(z)
    low_q = q_low[...]
    high_q = q_high[...]
    product = dot_nt(jnp.concatenate([z_high, z_low], axis=0), high_q)
    w = product[0:16] + product[16:32] + dot_nt(z_high, low_q) + base
    w = w.astype(bf16)
    nothing = jnp.zeros((16, 128), bf16)
    for q in range(4):
        pair = w[:, 128 * q : 128 * (q + 1)]
        left = jnp.concatenate([jnp.where(first, pair, nothing), jnp.where(first, nothing, pair)], axis=0)
        product = dot(left, basis[2 * q : 2 * q + 2].reshape(128, 256))
        out[2 * q] = out[2 * q] + product[0:16]
        out[2 * q + 1] = out[2 * q + 1] + product[16:32]

    for copy in halos:
        copy.wait_send()

    @pl.when(owner)
    def _():
        sent = parts_in.at[pl.ds(0, side * OWNERS - 1)]
        pltpu.make_async_copy(sent, sent, sum_send).wait()
        each_target(lambda z: pass_on(row_at, own_send.at[z], z).wait_send())
        rows = parts_in.at[pl.ds(0, group - 1)]
        pltpu.make_async_copy(rows, rows, z_send).wait()

    @pl.when(grp >= OWNERS)
    def _():
        sent = parts_in.at[pl.ds(0, side * OWNERS)]
        pltpu.make_async_copy(sent, sent, sum_send).wait()

    @pl.when(owner & (row_at == RELAY))
    def _():
        for i in range(2):
            for z in range(RELAY + 1, planes):
                pass_on(RELAY - 1 - i, relay_send.at[i, z], z).wait_send()


def solution(mesh):
    tops, group = mesh.shape["leaf"], mesh.shape["grp"]

    def body(vectors, leaf_basis, transfer, couple_src, couple_mat, root_src, root_mat, near_src, near_blocks):
        args = (
            vectors.transpose(0, 2, 1),
            leaf_basis.transpose(0, 2, 1),
            transfer.reshape(15, 64, 64),
            couple_mat.reshape(36, 64, 64),
            root_mat.reshape(4, 64, 64),
            near_blocks.transpose(0, 2, 1, 3),
            couple_src.transpose(2, 0, 1),
            root_src,
            near_src.transpose(1, 0),
        )
        hbm = pl.BlockSpec(memory_space=pltpu.HBM)
        dma = pltpu.SemaphoreType.DMA
        result = pl.pallas_call(
            functools.partial(kernel, tops, group, 8),
            out_shape=pltpu.VMEM((8, 16, 256), f32),
            in_specs=[hbm] * 9,
            out_specs=pl.BlockSpec(memory_space=pltpu.VMEM),
            scratch_shapes=[
                pltpu.VMEM((12, 16, 256), bf16),
                pltpu.VMEM((8, 64, 256), bf16),
                pltpu.VMEM((15, 64, 64), f32),
                pltpu.VMEM((36, 64, 64), f32),
                pltpu.VMEM((4, 64, 64), f32),
                pltpu.VMEM((8, 3, 256, 256), bf16),
                pltpu.SMEM((3, 1, 12), jnp.int32),
                pltpu.SMEM((1, 4), jnp.int32),
                pltpu.SMEM((3, 8), jnp.int32),
                pltpu.VMEM((14, 16, 128), bf16),
                pltpu.VMEM((10, 16, 128), bf16),
                pltpu.VMEM((4, 2, 128), f32),
                pltpu.VMEM((64, 2, 128), f32),
                pltpu.VMEM((tops, 2, 128), f32),
                pltpu.VMEM((4, 2, 128), f32),
                pltpu.VMEM((512, 128), bf16),
                pltpu.VMEM((512, 128), bf16),
                pltpu.VMEM((1536, 128), bf16),
                dma((9,)),
                dma((3,)),
                dma((6,)),
                dma((6,)),
                dma,
                dma,
                dma((8,)),
                dma((2, 8)),
                dma((8,)),
                dma,
                dma,
            ],
            compiler_params=pltpu.CompilerParams(
                collective_id=0, has_side_effects=True, vmem_limit_bytes=32 * 1024 * 1024
            ),
            name="h2",
        )(*(pltpu.with_memory_space_constraint(a, pltpu.HBM) for a in args))
        return result.transpose(0, 2, 1)

    both = ("leaf", "grp")
    in_specs = (
        P(both, None, None),
        P(both, None, None),
        P(both, None, None, None),
        P(both, None, None),
        P(both, None, None, None, None),
        P("leaf", None),
        P("leaf", None, None, None),
        P(both, None),
        P(both, None, None, None),
    )
    return jax.shard_map(body, mesh=mesh, in_specs=in_specs, out_specs=P(both, None, None), check_vma=False)
```

```python
import functools

import jax
import jax.numpy as jnp
from jax import lax
from jax.experimental import pallas as pl
from jax.experimental.pallas import tpu as pltpu
from jax.sharding import PartitionSpec as P

MESH = pl.DeviceIdType.MESH
f32, bf16 = jnp.float32, jnp.bfloat16
RELAY = 5
OWNERS = 2
ROWS = 8 // OWNERS
NT = (((1,), (1,)), ((), ()))


def dot(a, b):
    return jnp.dot(a, b, preferred_element_type=f32)


def dot_nt(a, b):
    return lax.dot_general(a, b, NT, preferred_element_type=f32)


def parts(x):
    high = x.astype(bf16)
    return high, (x - high.astype(f32)).astype(bf16)


def twice(x):
    return jnp.concatenate([x, x], axis=1)


def kernel(
    tops, group, side,
    v_hbm, b_hbm, t_hbm, c_hbm, r_hbm, n_hbm, cs_hbm, rs_hbm, ns_hbm,
    out,
    vext, basis, transfer, couple, root, near, cs, rs, ns,
    x0, x1, lifted_rows, parts_in, tops_in, z_rows, q_high, q_low, stack,
    in_sem, small_sem, halo_send, halo_recv, sum_send, sum_recv, own_send, relay_send, top_recv, z_send, z_recv,
):
    leaf, grp = lax.axis_index("leaf"), lax.axis_index("grp")
    devices = tops * group
    me = leaf * group + grp

    def load(src, dst, sem):
        copy = pltpu.make_async_copy(src, dst, sem)
        copy.start()
        return copy

    v_copy = load(v_hbm, vext.at[pl.ds(2, 8)], in_sem.at[0])
    b_copy = load(b_hbm, basis, in_sem.at[1])
    t_copy = load(t_hbm, transfer, in_sem.at[2])

    up, down = lax.rem(me + 1, devices), lax.rem(me + devices - 1, devices)
    up_id = (lax.div(up, group), lax.rem(up, group))
    down_id = (lax.div(down, group), lax.rem(down, group))
    barrier = pltpu.get_barrier_semaphore()

    def greet(device):
        pl.semaphore_signal(barrier, inc=1, device_id=device, device_id_type=MESH)

    def turn(i, n):
        return jnp.where(i >= n, i - n, i)

    def peer(o):
        return (leaf, turn(grp + o, group))

    row_at, column = lax.div(leaf, side), lax.rem(leaf, side)
    planes = tops // side
    plane = side * group
    place_in = column * group + grp

    def at(z):
        return (z * side + column, grp)

    def sends(z, t):
        return (z != t) & ((t <= RELAY) | ((z != RELAY - 1) & (z != RELAY - 2)))

    is_relayed = (row_at == RELAY - 1) | (row_at == RELAY - 2)
    targets = planes - 1 - jnp.where(is_relayed, planes - 1 - RELAY, 0)

    owner = grp < OWNERS

    def through_columns(act, count):
        @pl.loop(0, side - 1)
        def _(k):
            o = turn(k + side // 2, side)
            other = row_at * side + turn(column + jnp.where(k + side // 2 >= side, o + 1, o), side)
            for g in range(count):
                act((other, g), g)

    def owners_here(act):
        for g in range(OWNERS):
            pl.when(grp != g)(functools.partial(act, (leaf, g), g))

    @pl.when(owner)
    def _():
        through_columns(lambda device, g: greet(device), group)
        for o in range(1, group):
            greet(peer(o))
        for z in range(planes):
            pl.when(sends(z, row_at))(functools.partial(lambda z: greet(at(z)), z))

    @pl.when(grp >= OWNERS)
    def _():
        for g in range(OWNERS):
            greet((leaf, g))

    greet(up_id)
    greet(down_id)

    first = lax.broadcasted_iota(jnp.int32, (16, 128), 1) < 64
    first8 = lax.broadcasted_iota(jnp.int32, (8, 128), 1) < 64

    def split(x):
        high = x.astype(bf16).astype(f32)
        return jnp.where(first, high, x - high).astype(bf16)

    v_copy.wait()
    b_copy.wait()
    level = []
    for t in range(8):
        b = basis[t]
        x = split(dot_nt(vext[2 + t], jnp.concatenate([b, b], axis=0)))
        x0[3 + t] = x
        level.append(x)

    t_copy.wait()
    cs_copy = load(cs_hbm, cs, small_sem.at[0])
    rs_copy = load(rs_hbm, rs, small_sem.at[1])
    ns_copy = load(ns_hbm, ns, small_sem.at[2])
    r_copy = load(r_hbm, root, in_sem.at[3])
    n_copies = [load(n_hbm.at[pl.ds(2 * i, 2)], near.at[pl.ds(2 * i, 2)], in_sem.at[5 + i]) for i in range(4)]
    c_copy = load(c_hbm, couple, in_sem.at[4])
    e_high, e_low = [], []
    for i in range(15):
        high, low = parts(twice(transfer[i]))
        e_high.append(high)
        e_low.append(low)

    def lift(x, i):
        weights = jnp.concatenate([e_high[i], e_high[i], e_low[i], e_low[i]], axis=0)
        return dot(twice(x), weights)

    def chain(i, right):
        high, low = right
        e_h, e_l = e_high[i], e_low[i]
        left = jnp.where(lax.broadcasted_iota(jnp.int32, (64, 128), 1) < 64, e_h, e_l)
        return dot(twice(left), jnp.concatenate([high, high, low, low], axis=0))

    q2 = [parts(chain(12 + i, (e_high[14], e_low[14]))) for i in range(2)]
    offset = 0
    for height in range(1, 3):
        clusters = 16 >> height
        above = []
        for q in range(clusters // 2):
            x = split(lift(level[2 * q], offset + 2 * q) + lift(level[2 * q + 1], offset + 2 * q + 1))
            if height == 1:
                x1[3 + q] = x
            above.append(x)
        offset += clusters
        level = above
    top = None
    for x, (high, low) in zip(level, q2):
        term = dot(twice(x), jnp.concatenate([high, high, low, low], axis=0))
        top = term if top is None else top + term
    packed = jnp.where(first8, top[0:8], top[8:16])
    for i in range(OWNERS):
        lifted_rows[i] = packed[ROWS * i : ROWS * (i + 1)]

    pl.semaphore_wait(
        barrier, 2 + side * OWNERS + jnp.where(owner, group - OWNERS - 1 + targets, 0)
    )

    def hand_out(device, g):
        pltpu.make_async_remote_copy(
            lifted_rows.at[g], parts_in.at[place_in], sum_send, sum_recv, device, MESH
        ).start()

    through_columns(hand_out, OWNERS)
    owners_here(hand_out)

    @pl.when(owner)
    def _():
        parts_in[place_in] = lifted_rows[grp]

    halos = []

    def halo(src, dst, n, device):
        copy = pltpu.make_async_remote_copy(src, dst, halo_send.at[n], halo_recv.at[n], device, MESH)
        copy.start()
        halos.append(copy)

    halo(vext.at[pl.ds(8, 2)], vext.at[pl.ds(0, 2)], 0, up_id)
    halo(vext.at[pl.ds(2, 2)], vext.at[pl.ds(10, 2)], 1, down_id)
    halo(x0.at[pl.ds(8, 3)], x0.at[pl.ds(0, 3)], 2, up_id)
    halo(x0.at[pl.ds(3, 3)], x0.at[pl.ds(11, 3)], 3, down_id)
    halo(x1.at[pl.ds(4, 3)], x1.at[pl.ds(0, 3)], 4, up_id)
    halo(x1.at[pl.ds(3, 3)], x1.at[pl.ds(7, 3)], 5, down_id)

    q1 = [parts(chain(8 + i, q2[i // 2])) for i in range(4)]
    for c in range(8):
        high, low = parts(chain(c, q1[c // 2]))
        q_high[pl.ds(64 * c, 64)] = high
        q_low[pl.ds(64 * c, 64)] = low

    r_copy.wait()
    highs, lows = [], []
    for j in range(4):
        m = root[j]
        zero = jnp.zeros_like(m)
        diagonal = jnp.concatenate([jnp.concatenate([m, zero], axis=1), jnp.concatenate([zero, m], axis=1)], axis=0)
        high, low = parts(diagonal)
        highs.append(high)
        lows.append(low)
    stack[...] = jnp.concatenate(highs + highs + lows, axis=0)
    for i in range(4):
        n_copies[i].wait()
        for t in range(2 * i, 2 * i + 2):
            out[t] = dot_nt(vext[2 + t], near[t, 0])

    def block(z):
        return tops_in.at[pl.ds(z * side, side)]

    def pass_on(z, send, target):
        return pltpu.make_async_remote_copy(block(z), block(z), send, top_recv.at[z], at(target), MESH)

    def arrive(z):
        pltpu.make_async_copy(block(z), block(z), top_recv.at[z]).wait()

    def each_target(act):
        for z in range(planes):
            pl.when(sends(row_at, z))(functools.partial(act, z))

    @pl.when(owner)
    def _():
        others = parts_in.at[pl.ds(0, plane - 1)]
        pltpu.make_async_copy(others, others, sum_recv).wait()
        tops_in[pl.ds(row_at * side, side)] = parts_in[...].reshape(side, group, ROWS, 128).sum(axis=1)
        each_target(lambda z: pass_on(row_at, own_send.at[z], z).start())

    @pl.when(owner & (row_at == RELAY))
    def _():
        for i in range(2):
            arrive(RELAY - 1 - i)
            for z in range(RELAY + 1, planes):
                pass_on(RELAY - 1 - i, relay_send.at[i, z], z).start()

    rs_copy.wait()
    ns_copy.wait()
    cs_copy.wait()
    for copy in halos:
        copy.wait_recv()
    for t in range(8):
        total = out[t]
        for e in range(1, 3):
            place = jnp.minimum(jnp.bitwise_and(ns[e, t] - 8 * me + 2, 8 * devices - 1), 11)
            total = total + dot_nt(vext[place], near[t, e])
        out[t] = total

    c_copy.wait()

    def coupling(x, row, base, cycle):
        total = None
        for j in range(3):
            place = jnp.minimum(jnp.bitwise_and(cs[j, 0, row] - base + 3, cycle - 1), x.shape[0] - 1)
            high, low = parts(couple[3 * row + j])
            term = dot(twice(x[place]), jnp.concatenate([high, high, low, low], axis=0))
            total = term if total is None else total + term
        return total

    pairs = []
    for q in range(4):
        y1 = split(twice(coupling(x1, 8 + q, 4 * me, 4 * devices)))
        weights = jnp.concatenate(
            [
                jnp.concatenate([e_high[2 * q], e_low[2 * q]], axis=1),
                jnp.concatenate([e_high[2 * q + 1], e_low[2 * q + 1]], axis=1),
            ],
            axis=0,
        )
        y0 = [coupling(x0, 2 * q + i, 8 * me, 8 * devices) for i in range(2)]
        pairs.append(dot_nt(twice(y1), weights) + jnp.concatenate(y0, axis=1))
    base = jnp.concatenate(pairs, axis=1)

    @pl.when(owner)
    def _():
        for z in range(planes):
            expected = row_at != z
            if z in (RELAY - 1, RELAY - 2):
                expected = expected & (row_at != RELAY)
            pl.when(expected)(functools.partial(arrive, z))
        g = jnp.concatenate([tops_in[jnp.bitwise_and(rs[0, j], tops - 1)] for j in range(4)], axis=1)
        high, low = parts(g)
        z_rows[grp] = dot(jnp.concatenate([high, low, high], axis=1), stack[...])
        for o in range(1, group):
            pltpu.make_async_remote_copy(z_rows.at[grp], z_rows.at[grp], z_send, z_recv, peer(o), MESH).start()
        others = z_rows.at[pl.ds(0, OWNERS - 1)]
        pltpu.make_async_copy(others, others, z_recv).wait()

    @pl.when(grp >= OWNERS)
    def _():
        pltpu.make_async_copy(z_rows, z_rows, z_recv).wait()

    z = jnp.concatenate([z_rows[i] for i in range(OWNERS)], axis=0)
    zero = jnp.zeros_like(z)
    z = jnp.concatenate([jnp.where(first8, z, zero), jnp.where(first8, zero, z)], axis=0)
    z_high, z_low = parts(z)
    low_q = q_low[...]
    high_q = q_high[...]
    product = dot_nt(jnp.concatenate([z_high, z_low], axis=0), high_q)
    w = product[0:16] + product[16:32] + dot_nt(z_high, low_q) + base
    w = w.astype(bf16)
    nothing = jnp.zeros((16, 128), bf16)
    for q in range(4):
        pair = w[:, 128 * q : 128 * (q + 1)]
        left = jnp.concatenate([jnp.where(first, pair, nothing), jnp.where(first, nothing, pair)], axis=0)
        product = dot(left, basis[2 * q : 2 * q + 2].reshape(128, 256))
        out[2 * q] = out[2 * q] + product[0:16]
        out[2 * q + 1] = out[2 * q + 1] + product[16:32]

    for copy in halos:
        copy.wait_send()

    @pl.when(owner)
    def _():
        sent = parts_in.at[pl.ds(0, side * OWNERS - 1)]
        pltpu.make_async_copy(sent, sent, sum_send).wait()
        each_target(lambda z: pass_on(row_at, own_send.at[z], z).wait_send())
        rows = parts_in.at[pl.ds(0, group - 1)]
        pltpu.make_async_copy(rows, rows, z_send).wait()

    @pl.when(grp >= OWNERS)
    def _():
        sent = parts_in.at[pl.ds(0, side * OWNERS)]
        pltpu.make_async_copy(sent, sent, sum_send).wait()

    @pl.when(owner & (row_at == RELAY))
    def _():
        for i in range(2):
            for z in range(RELAY + 1, planes):
                pass_on(RELAY - 1 - i, relay_send.at[i, z], z).wait_send()


def solution(mesh):
    tops, group = mesh.shape["leaf"], mesh.shape["grp"]

    def body(vectors, leaf_basis, transfer, couple_src, couple_mat, root_src, root_mat, near_src, near_blocks):
        args = (
            vectors.transpose(0, 2, 1),
            leaf_basis.transpose(0, 2, 1),
            transfer.reshape(15, 64, 64),
            couple_mat.reshape(36, 64, 64),
            root_mat.reshape(4, 64, 64),
            near_blocks.transpose(0, 2, 1, 3),
            couple_src.transpose(2, 0, 1),
            root_src,
            near_src.transpose(1, 0),
        )
        hbm = pl.BlockSpec(memory_space=pltpu.HBM)
        dma = pltpu.SemaphoreType.DMA
        result = pl.pallas_call(
            functools.partial(kernel, tops, group, 8),
            out_shape=pltpu.VMEM((8, 16, 256), f32),
            in_specs=[hbm] * 9,
            out_specs=pl.BlockSpec(memory_space=pltpu.VMEM),
            scratch_shapes=[
                pltpu.VMEM((12, 16, 256), bf16),
                pltpu.VMEM((8, 64, 256), bf16),
                pltpu.VMEM((15, 64, 64), f32),
                pltpu.VMEM((36, 64, 64), f32),
                pltpu.VMEM((4, 64, 64), f32),
                pltpu.VMEM((8, 3, 256, 256), bf16),
                pltpu.SMEM((3, 1, 12), jnp.int32),
                pltpu.SMEM((1, 4), jnp.int32),
                pltpu.SMEM((3, 8), jnp.int32),
                pltpu.VMEM((14, 16, 128), bf16),
                pltpu.VMEM((10, 16, 128), bf16),
                pltpu.VMEM((OWNERS, ROWS, 128), f32),
                pltpu.VMEM((64, ROWS, 128), f32),
                pltpu.VMEM((tops, ROWS, 128), f32),
                pltpu.VMEM((OWNERS, ROWS, 128), f32),
                pltpu.VMEM((512, 128), bf16),
                pltpu.VMEM((512, 128), bf16),
                pltpu.VMEM((1536, 128), bf16),
                dma((9,)),
                dma((3,)),
                dma((6,)),
                dma((6,)),
                dma,
                dma,
                dma((8,)),
                dma((2, 8)),
                dma((8,)),
                dma,
                dma,
            ],
            compiler_params=pltpu.CompilerParams(
                collective_id=0, has_side_effects=True, vmem_limit_bytes=32 * 1024 * 1024
            ),
            name="h2",
        )(*(pltpu.with_memory_space_constraint(a, pltpu.HBM) for a in args))
        return result.transpose(0, 2, 1)

    both = ("leaf", "grp")
    in_specs = (
        P(both, None, None),
        P(both, None, None),
        P(both, None, None, None),
        P(both, None, None),
        P(both, None, None, None, None),
        P("leaf", None),
        P("leaf", None, None, None),
        P(both, None),
        P(both, None, None, None),
    )
    return jax.shard_map(body, mesh=mesh, in_specs=in_specs, out_specs=P(both, None, None), check_vma=False)
```
